256 devices in a mesh: rep: 8 (over x, y_lo), fsdp: 32 (over y_hi, z, core).
Axes of the slice: x: 4, y: 4 (y_hi: 2, y_lo: 2; y = y_hi * 2 + y_lo), z: 8, core: 2. Of those that a mesh axis runs over, the one named last changes fastest.
Arguments:
- tokens: bfloat16 [4096, 4096], P('rep'), may hold values from -40 to 40
- norm_gain: float32 [4096], replicated, may hold values from 0.1 to 1.9
- gate_weight: bfloat16 [8, 4096, 7168], P('rep', None, 'fsdp'), may hold values from -6 to 6
- up_weight: bfloat16 [8, 4096, 7168], P('rep', None, 'fsdp'), may hold values from -6 to 6
- down_weight: bfloat16 [8, 7168, 4096], P('rep', 'fsdp'), may hold values from -6 to 6
- outer_block: float32 [7168, 4096], P('fsdp', 'rep'), may hold values from -6 to 6
- momentum: float32 [7168, 4096], P('fsdp', 'rep'), may hold values from -6 to 6
- cotangent: bfloat16 [4096, 4096], P('rep'), may hold values from -6 to 6
Outputs:
- mixed: bfloat16 [4096, 4096], P(('rep', 'fsdp'))
- input_grad: bfloat16 [4096, 4096], P(('rep', 'fsdp'))
- new_outer: float32 [7168, 4096], P('fsdp', 'rep')
- new_momentum: float32 [7168, 4096], P('fsdp', 'rep')
The draws below stay inside these ranges and needn't reach their ends.
All inputs are finite; a program needn't handle non-finite values.
Results may differ from the reference program's by a relative error of at most 0.0065.
Values sent between devices are 32-bit elements; how exact they have to be, the bound alone decides.
A program may use at most 128 MiB of HBM per device.

```python
import math
import jax
import jax.numpy as jnp
from jax import lax

D = 4096
FFW = 7168
GROUP = 512
TOKENS = 4096
N_REP = 8


def draw_tokens(key, part):
    key = jax.random.fold_in(key, 11)
    base_key, row_key, col_key = jax.random.split(key, 3)
    base = jax.random.truncated_normal(base_key, -4.0, 4.0, (TOKENS, D), jnp.float32)
    row_scale = jnp.exp(jax.random.uniform(row_key, (TOKENS, 1), jnp.float32, math.log(0.25), math.log(2.5)))
    col_scale = jnp.exp(jax.random.uniform(col_key, (1, D), jnp.float32, math.log(0.4), math.log(4.0)))
    return (base * row_scale * col_scale).astype(jnp.bfloat16)


def with_spikes(result, rng, source, target, shards_of, factor):
    owner, partner = [(jnp.arange(result.shape[position]) // (result.shape[position] // shards_of)).reshape([-1 if axis == position else 1 for axis in range(result.ndim)]) for position in (source, target)]
    chosen = jax.random.permutation(rng, shards_of)[partner]
    strong = (owner == chosen) | (owner == (partner + shards_of // 2) % shards_of)
    return jnp.where(strong, factor * result, result)


def steps_of(stream_key, shape, shards, smallest, high):
    level, own = 1.0, jax.random.fold_in(stream_key, 6)
    for position, parts in shards:
        draws = jnp.exp(jax.random.uniform(jax.random.fold_in(own, position), (parts,), jnp.float32, smallest / len(shards), high / len(shards)))
        level = level * jnp.repeat(draws, shape[position] // parts).reshape([-1 if axis == position else 1 for axis in range(len(shape))])
    return level


def noise(stream_key, extent, spread, most, pieces=(), dtype=jnp.bfloat16):
    array = spread * jax.random.normal(stream_key, extent, jnp.float32)
    if pieces:
        array = array * steps_of(stream_key, extent, pieces, -0.22, 0.18)
    return jnp.clip(array, -most, most).astype(dtype)


def gaussian_with(stream_key, shape, deviation, most, cuts, heavy, held_as=jnp.bfloat16):
    entries = deviation * jax.random.normal(stream_key, shape, jnp.float32)
    if cuts:
        entries = entries * steps_of(stream_key, shape, cuts, -0.22, 0.18)
    return jnp.clip(with_spikes(entries, jax.random.fold_in(stream_key, 3), *heavy), -most, most).astype(held_as)


def setup_inputs(seed: int = 0) -> dict:
    key_list = jax.random.split(jax.random.key(seed), 9)
    tokens = draw_tokens(jax.random.fold_in(key_list[8], 71), 0)
    norm_gain = jnp.clip(1.0 + 0.18 * jax.random.normal(key_list[1], (D,), jnp.float32), 0.1, 1.9)
    gate_weight = noise(key_list[2], (N_REP, D, FFW), 1.0, 6.0, ((0, 8), (2, 32)))
    up_weight = noise(key_list[3], (N_REP, D, FFW), 1.0, 6.0, ((0, 8), (2, 32)))
    down_weight = gaussian_with(key_list[4], (N_REP, FFW, D), 1.0, 6.0, ((0, 8), (1, 32)), (0, 2, 8, 2.0))
    outer_block = noise(key_list[5], (FFW, D), 1.0, 6.0, ((0, 32), (1, 8)), jnp.float32)
    momentum = noise(key_list[6], (FFW, D), 1.0, 6.0, ((0, 32), (1, 8)), jnp.float32)
    cotangent = noise(key_list[7], (TOKENS, D), 1.0, 6.0, ((0, 8),))
    return {"tokens": tokens, "norm_gain": norm_gain, "gate_weight": gate_weight, "up_weight": up_weight, "down_weight": down_weight, "outer_block": outer_block, "momentum": momentum, "cotangent": cotangent}


def reference(tokens, norm_gain, gate_weight, up_weight, down_weight, outer_block, momentum, cotangent):
    scale_in = D ** (-0.5)
    scale_out = FFW ** (-0.5)
    rows32 = tokens.astype(jnp.float32).reshape(N_REP, GROUP, D)
    upstream = cotangent.reshape(N_REP, GROUP, D)
    inverse = lax.rsqrt(lax.optimization_barrier(jnp.mean(rows32 * rows32, axis=-1, keepdims=True)) + 1e-05)
    plain = rows32 * inverse
    normed = (plain * norm_gain).astype(jnp.bfloat16)
    outputs = []
    grads = []
    total = jnp.zeros((FFW, D), jnp.float32)
    for replica in range(N_REP):
        gate = jnp.dot(normed[replica], gate_weight[replica], preferred_element_type=jnp.float32) * scale_in
        up = jnp.dot(normed[replica], up_weight[replica], preferred_element_type=jnp.float32) * scale_in
        sig = jax.nn.sigmoid(gate)
        act = gate * sig
        hidden = (act * up).astype(jnp.bfloat16)
        branch = jnp.dot(hidden, down_weight[replica], preferred_element_type=jnp.float32) * scale_out
        outputs.append(branch.astype(jnp.bfloat16))
        d_hidden = jnp.dot(upstream[replica], down_weight[replica].T, preferred_element_type=jnp.float32) * scale_out
        d_gate = (d_hidden * up * sig * (1.0 + gate * (1.0 - sig))).astype(jnp.bfloat16)
        d_up = (d_hidden * act).astype(jnp.bfloat16)
        d_normed = (jnp.dot(d_gate, gate_weight[replica].T, preferred_element_type=jnp.float32) + jnp.dot(d_up, up_weight[replica].T, preferred_element_type=jnp.float32)) * scale_in
        scaled = d_normed * norm_gain
        centre = lax.optimization_barrier(jnp.mean(scaled * plain[replica], axis=-1, keepdims=True))
        grads.append((inverse[replica] * (scaled - plain[replica] * centre)).astype(jnp.bfloat16))
        grad_down = jnp.dot(hidden.T, upstream[replica], preferred_element_type=jnp.float32) * scale_out
        total = total + (down_weight[replica].astype(jnp.float32) - 0.5 * grad_down)
    pseudo = outer_block - total / N_REP
    new_momentum = 0.9 * momentum + pseudo
    new_outer = outer_block - 0.7 * (pseudo + 0.9 * new_momentum)
    mixed = jnp.concatenate(outputs, axis=0)
    input_grad = jnp.concatenate(grads, axis=0)
    return (mixed, input_grad, new_outer, new_momentum)
```

```python
import jax
import jax.numpy as jnp
from jax import lax
from jax.experimental import pallas as pl
from jax.experimental.pallas import tpu as pltpu
from jax.sharding import PartitionSpec as P

D = 4096
FFW = 7168
N_REP = 8
MESH = pl.DeviceIdType.MESH
F32 = jnp.float32
BF16 = jnp.bfloat16

NZ = 8
CA = 1280
CB = 768
A_COLS = (pl.ds(0, CA), pl.ds(CA, CA))
B_COLS = (pl.ds(2 * CA, CB), pl.ds(2 * CA + CB, CB))
A_ALL = pl.ds(0, 2 * CA)
B_ALL = pl.ds(2 * CA, 2 * CB)
SCALE_IN = D ** (-0.5)
SCALE_OUT = FFW ** (-0.5)
T0 = (((1,), (1,)), ((), ()))


def slot_of(direction, step):
    if step == NZ - 1:
        return 7
    if direction == 0:
        return 2 * step if step <= 3 else 13 - 2 * step
    return 2 * step + 1 if step <= 2 else 12 - 2 * step


OFFSETS = (-1, 1, -2, 2, -3, 3, 4, 0)


def kernel(
    tokens, gain_hbm, gate_hbm, up_hbm, down_hbm, outer_hbm, mom_hbm, cot_hbm,
    mixed_out, grad_out, outer_out, mom_out,
    tok, cot, wg, wu, wd, gain, own_tok, outer, mom,
    gate_s, up_s, hid, hid_t,
    own, peer, prec, g, arec, brec, yrec, frec, xrec, lrec,
    load_sem, tok_sem, cot_sem,
    p_sem, a_send, a_recv, b_send, b_recv, y_send, y_recv, f_sem, x_send, x_recv, l_sem,
):
    r = lax.axis_index("rep")
    f = lax.axis_index("fsdp")
    x, yl = r // 2, lax.rem(r, 2)
    yh, z, c = f // 16, lax.rem(f // 2, NZ), lax.rem(f, 2)

    def at(yh_, z_, c_):
        return (yh_ * NZ + z_) * 2 + c_

    pair = (r, at(yh, z, 1 - c))
    z_next = ((r, at(yh, lax.rem(z + 1, NZ), c)), (r, at(yh, lax.rem(z + NZ - 1, NZ), c)))
    y_peer = (r, at(1 - yh, z, c))
    x_next = ((lax.rem(x + 1, 4) * 2 + yl, f), (lax.rem(x + 3, 4) * 2 + yl, f))
    l_peer = (x * 2 + 1 - yl, f)

    barrier = pltpu.get_barrier_semaphore()
    for other in (pair, *z_next, y_peer, *x_next, l_peer):
        pl.semaphore_signal(barrier, inc=1, device_id=other, device_id_type=MESH)

    def load_rows(src, dst, sem, k):
        for h in range(2):
            for jj in range(2):
                for yp in range(2):
                    zz = lax.rem(z + OFFSETS[2 * k + jj] + NZ, NZ)
                    cc = c if h else 1 - c
                    yy = yh if yp else 1 - yh
                    row = pl.multiple_of(at(yy, zz, cc) * 16, 16)
                    pltpu.make_async_copy(
                        src.at[pl.ds(row, 16), :],
                        dst.at[pl.ds(k * 128 + h * 64 + jj * 32 + yp * 16, 16), :],
                        sem.at[k],
                    ).start()

    def wait_rows(dst, sem, k):
        block = dst.at[pl.ds(k * 128, 128), :]
        pltpu.make_async_copy(block, block, sem.at[k]).wait()

    loads = [
        pltpu.make_async_copy(gain_hbm, gain, load_sem.at[0]),
        pltpu.make_async_copy(gate_hbm.at[0], wg, load_sem.at[1]),
        pltpu.make_async_copy(up_hbm.at[0], wu, load_sem.at[2]),
        pltpu.make_async_copy(down_hbm.at[0], wd, load_sem.at[3]),
        pltpu.make_async_copy(
            tokens.at[pl.ds(pl.multiple_of(f * 16, 16), 16), :], own_tok, load_sem.at[4]
        ),
        pltpu.make_async_copy(outer_hbm, outer, load_sem.at[5]),
        pltpu.make_async_copy(mom_hbm, mom, load_sem.at[6]),
    ]
    loads[0].start()
    load_rows(tokens, tok, tok_sem, 0)
    for i in (1, 2, 3):
        loads[i].start()
    for k in (1, 2, 3):
        load_rows(tokens, tok, tok_sem, k)
    for k in range(4):
        load_rows(cot_hbm, cot, cot_sem, k)
    for i in (4, 5, 6):
        loads[i].start()

    sends = []

    def remote(src, dst, ssem, rsem, to):
        copy = pltpu.make_async_remote_copy(
            src_ref=src, dst_ref=dst, send_sem=ssem, recv_sem=rsem, device_id=to, device_id_type=MESH
        )
        copy.start()
        sends.append(copy)
        return copy

    def front(k):
        wait_rows(tok, tok_sem, k)
        if k == 0:
            loads[0].wait()

        @pl.loop(0, 8)
        def _(i):
            rows = pl.ds(pl.multiple_of(k * 128 + i * 16, 16), 16)
            part = tok[rows, :].astype(F32)
            inverse = lax.rsqrt(jnp.mean(part * part, axis=1, keepdims=True) + 1e-05)
            tok[rows, :] = (part * inverse * gain[...]).astype(BF16)

        if k == 0:
            loads[1].wait()
            loads[2].wait()
        rows = pl.ds(k * 128, 128)
        normed = tok[rows, :]
        gate = jnp.dot(normed, wg[...], preferred_element_type=F32) * SCALE_IN
        up = jnp.dot(normed, wu[...], preferred_element_type=F32) * SCALE_IN
        gate_s[rows, :] = gate
        up_s[rows, :] = up
        sig = 1.0 / (1.0 + jnp.exp(-gate))
        hid[rows, :] = (gate * sig * up).astype(BF16)

    def put(a, k, cols, value):
        peer[a, pl.ds(k * 64, 64), cols] = value[:64]
        own[a, pl.ds(k * 64, 64), cols] = value[64:]

    def mix(k):
        if k == 0:
            loads[3].wait()
        hidden = hid[pl.ds(k * 128, 128), :]

        @pl.loop(0, 8)
        def _(n):
            cols = pl.ds(pl.multiple_of(n * 512, 512), 512)
            put(0, k, cols, jnp.dot(hidden, wd[:, cols], preferred_element_type=F32))

    def back(k):
        rows = pl.ds(k * 128, 128)
        d_hidden = lax.dot_general(cot[rows, :], wd[...], T0, preferred_element_type=F32) * SCALE_OUT
        gate = gate_s[rows, :]
        up = up_s[rows, :]
        sig = 1.0 / (1.0 + jnp.exp(-gate))
        d_gate = (d_hidden * up * sig * (1.0 + gate * (1.0 - sig))).astype(BF16)
        d_up = (d_hidden * (gate * sig)).astype(BF16)

        @pl.loop(0, 8)
        def _(n):
            cols = pl.ds(pl.multiple_of(n * 512, 512), 512)
            first = lax.dot_general(d_gate, wg[cols, :], T0, preferred_element_type=F32)
            second = lax.dot_general(d_up, wu[cols, :], T0, preferred_element_type=F32)
            put(1, k, cols, first + second)

    def grad(q):
        step, side = q // 2, q % 2
        xx = lax.rem(x + 4 + (step + 1 if side else -(step + 1)), 4)
        col = pl.multiple_of((xx * 2 + (yl if side else 1 - yl)) * 512, 512)
        cols = pl.ds(col, 512)
        down_grad = jnp.dot(hid_t[...], cot[:, cols], preferred_element_type=F32)
        g[q] = wd[:, cols].astype(F32) - (0.5 * SCALE_OUT) * down_grad

    pairs, rings_a, rings_b, ys, finals, xs = {}, {}, {}, {}, {}, {}

    def pair_send(a, k):
        rows = pl.ds(k * 64, 64)
        pairs[a, k] = remote(
            peer.at[a, rows, :], prec.at[a, rows, :], p_sem.at[0, a, k], p_sem.at[1, a, k], pair
        )

    def pair_add(a, k):
        pairs[a, k].wait_recv()
        rows = pl.ds(k * 64, 64)

        @pl.loop(0, 8)
        def _(n):
            cols = pl.ds(pl.multiple_of(n * 512, 512), 512)
            own[a, rows, cols] += prec[a, rows, cols]

    def y_start(a, k):
        for j in (2 * k, 2 * k + 1):
            ys[a, j] = remote(
                own.at[a, pl.ds(j * 32, 16), B_ALL], yrec.at[a, j],
                y_send.at[a, j], y_recv.at[a, j], y_peer,
            )

    def y_add(a, k):
        for j in (2 * k, 2 * k + 1):
            ys[a, j].wait_recv()
            own[a, pl.ds(j * 32 + 16, 16), B_ALL] += yrec[a, j]

    def ring_a(a, step):
        for d in range(2):
            rows = pl.ds(slot_of(d, step) * 32, 32)
            if step:
                rings_a[a, d, step - 1].wait_recv()
                own[a, rows, A_COLS[d]] += arec[a, d, step - 1]
            if step < NZ - 1:
                rings_a[a, d, step] = remote(
                    own.at[a, rows, A_COLS[d]], arec.at[a, d, step],
                    a_send.at[a, d, step], a_recv.at[a, d, step], z_next[d],
                )

    def ring_b(a, step):
        for d in range(2):
            rows = pl.ds(slot_of(d, step) * 32 + 16, 16)
            if step:
                rings_b[a, d, step - 1].wait_recv()
                own[a, rows, B_COLS[d]] += brec[a, d, step - 1]
            if step < NZ - 1:
                rings_b[a, d, step] = remote(
                    own.at[a, rows, B_COLS[d]], brec.at[a, d, step],
                    b_send.at[a, d, step], b_recv.at[a, d, step], z_next[d],
                )

    def final_start(a):
        ring_a(a, NZ - 1)
        finals[a] = remote(
            own.at[a, pl.ds(224, 16), A_ALL], frec.at[a], f_sem.at[0, a], f_sem.at[1, a], y_peer
        )

    def final_add(a):
        finals[a].wait_recv()
        own[a, pl.ds(240, 16), A_ALL] += frec[a]

    def x_step(step):
        for d in range(2):
            if step:
                xs[d, step - 1].wait_recv()
                g[2 * step + d] += xrec[d, step - 1]
            if step < 3:
                xs[d, step] = remote(
                    g.at[2 * step + d], xrec.at[d, step], x_send.at[d, step], x_recv.at[d, step], x_next[d]
                )
        if step == 3:
            xs["l"] = remote(g.at[6], lrec, l_sem.at[0], l_sem.at[1], l_peer)

    front(0)
    pl.semaphore_wait(barrier, 7)
    mix(0)
    pair_send(0, 0)
    front(1)
    pair_add(0, 0)
    ring_a(0, 0)
    y_start(0, 0)
    mix(1)
    pair_send(0, 1)
    front(2)
    pair_add(0, 1)
    ring_a(0, 1)
    y_start(0, 1)
    y_add(0, 0)
    ring_b(0, 0)
    mix(2)
    pair_send(0, 2)
    front(3)
    pair_add(0, 2)
    ring_a(0, 2)
    y_start(0, 2)
    y_add(0, 1)
    ring_b(0, 1)
    mix(3)
    pair_send(0, 3)
    hid_t[...] = hid[...].T
    for k in range(4):
        wait_rows(cot, cot_sem, k)
    grad(0)
    grad(1)
    x_step(0)
    pair_add(0, 3)
    ring_a(0, 3)
    y_start(0, 3)
    y_add(0, 2)
    ring_b(0, 2)
    for q in range(2, 8):
        grad(q)
    back(0)
    pair_send(1, 0)
    ring_a(0, 4)
    y_add(0, 3)
    ring_b(0, 3)
    back(1)
    pair_send(1, 1)
    pair_add(1, 0)
    ring_a(1, 0)
    y_start(1, 0)
    ring_a(0, 5)
    ring_b(0, 4)
    x_step(1)
    back(2)
    pair_send(1, 2)
    pair_add(1, 1)
    ring_a(1, 1)
    y_start(1, 1)
    ring_a(0, 6)
    ring_b(0, 5)
    y_add(1, 0)
    ring_b(1, 0)
    back(3)
    pair_send(1, 3)
    pair_add(1, 2)
    ring_a(1, 2)
    y_start(1, 2)
    final_start(0)
    ring_b(0, 6)
    y_add(1, 1)
    ring_b(1, 1)
    x_step(2)
    pair_add(1, 3)
    ring_a(1, 3)
    y_start(1, 3)
    ring_b(0, 7)
    y_add(1, 2)
    ring_b(1, 2)
    final_add(0)
    mixed_out[...] = (own[0, pl.ds(240, 16), :] * SCALE_OUT).astype(BF16)
    ring_a(1, 4)
    y_add(1, 3)
    ring_b(1, 3)
    x_step(3)
    ring_a(1, 5)
    ring_b(1, 4)
    ring_a(1, 6)
    ring_b(1, 5)
    final_start(1)
    ring_b(1, 6)
    ring_b(1, 7)
    final_add(1)

    loads[4].wait()
    part = own_tok[...].astype(F32)
    inverse = lax.rsqrt(jnp.mean(part * part, axis=1, keepdims=True) + 1e-05)
    plain = part * inverse
    scaled = own[1, pl.ds(240, 16), :] * SCALE_IN * gain[...]
    centre = jnp.mean(scaled * plain, axis=1, keepdims=True)
    grad_out[...] = (inverse * (scaled - plain * centre)).astype(BF16)

    loads[5].wait()
    loads[6].wait()
    xs["l"].wait_recv()
    total = g[7] + lrec[...]
    pseudo = outer[...] - total * (1.0 / N_REP)
    new_momentum = 0.9 * mom[...] + pseudo
    mom_out[...] = new_momentum
    outer_out[...] = outer[...] - 0.7 * (pseudo + 0.9 * new_momentum)

    for copy in sends:
        copy.wait_send()


def body(tokens, norm_gain, gate_weight, up_weight, down_weight, outer_block, momentum, cotangent):
    units = down_weight.shape[1]
    cols = outer_block.shape[1]
    hbm = pl.BlockSpec(memory_space=pl.ANY)
    vmem = pl.BlockSpec(memory_space=pltpu.VMEM)
    dma = pltpu.SemaphoreType.DMA
    v = pltpu.VMEM
    return pl.pallas_call(
        kernel,
        name="window",
        out_shape=(
            jax.ShapeDtypeStruct((16, D), BF16),
            jax.ShapeDtypeStruct((16, D), BF16),
            jax.ShapeDtypeStruct((units, cols), F32),
            jax.ShapeDtypeStruct((units, cols), F32),
        ),
        in_specs=[hbm] * 8,
        out_specs=(vmem,) * 4,
        scratch_shapes=[
            v((512, D), BF16), v((512, D), BF16), v((D, units), BF16), v((D, units), BF16),
            v((units, D), BF16), v((1, D), F32), v((16, D), BF16), v((units, cols), F32), v((units, cols), F32),
            v((512, units), F32), v((512, units), F32), v((512, units), BF16), v((units, 512), BF16),
            v((2, 256, D), F32), v((2, 256, D), F32), v((2, 256, D), F32), v((8, units, cols), F32),
            v((2, 2, 7, 32, CA), F32), v((2, 2, 7, 16, CB), F32), v((2, 8, 16, 2 * CB), F32),
            v((2, 16, 2 * CA), F32), v((2, 3, units, cols), F32), v((units, cols), F32),
            dma((7,)), dma((4,)), dma((4,)),
            dma((2, 2, 4)), dma((2, 2, 7)), dma((2, 2, 7)), dma((2, 2, 7)), dma((2, 2, 7)),
            dma((2, 8)), dma((2, 8)), dma((2, 2)), dma((2, 3)), dma((2, 3)), dma((2,)),
        ],
        compiler_params=pltpu.CompilerParams(
            collective_id=0, has_side_effects=True, vmem_limit_bytes=63 * 2**20
        ),
    )(tokens, norm_gain.reshape(1, D), gate_weight, up_weight, down_weight, outer_block, momentum, cotangent)


def solution(mesh):
    placed = (
        P("rep", None),
        P(),
        P("rep", None, "fsdp"),
        P("rep", None, "fsdp"),
        P("rep", "fsdp", None),
        P("fsdp", "rep"),
        P("fsdp", "rep"),
        P("rep", None),
    )
    return jax.shard_map(
        body,
        mesh=mesh,
        in_specs=placed,
        out_specs=(
            P(("rep", "fsdp"), None),
            P(("rep", "fsdp"), None),
            P("fsdp", "rep"),
            P("fsdp", "rep"),
        ),
        check_vma=False,
    )
```

```python
import jax
import jax.numpy as jnp
from jax import lax
from jax.experimental import pallas as pl
from jax.experimental.pallas import tpu as pltpu
from jax.sharding import PartitionSpec as P

D = 4096
FFW = 7168
N_REP = 8
MESH = pl.DeviceIdType.MESH
F32 = jnp.float32
BF16 = jnp.bfloat16

NZ = 8
CA = (1152, 768)
CB = (896, 1280)
SCALE_IN = D ** (-0.5)
SCALE_OUT = FFW ** (-0.5)
NT = (((1,), (1,)), ((), ()))
OFFSETS = (-1, 1, -2, 2, -3, 3, 4, 0)


def groups(a):
    return ((0, CA[a]), (CA[a], CA[a]), (2 * CA[a], CB[a]), (2 * CA[a] + CB[a], CB[a]))


def pieces(start, size):
    return [(start + i, min(512, size - i)) for i in range(0, size, 512)]


def slot_of(direction, step):
    if step == NZ - 1:
        return 7
    if direction == 0:
        return 2 * step if step <= 3 else 13 - 2 * step
    return 2 * step + 1 if step <= 2 else 12 - 2 * step


def kernel(
    tokens, gain_hbm, gate_hbm, up_hbm, down_hbm, outer_hbm, mom_hbm, cot_hbm,
    mixed_out, grad_out, outer_out, mom_out,
    tok, cot, wg, wu, wd, gain, own_tok, outer, mom, mixed_v, grad_v,
    gate_s, up_s, hid, hid_t,
    own, peer, prec, g, arec0, arec1, brec0, brec1, yrec0, yrec1, frec0, frec1, xrec, lrec,
    load_sem, tok_sem, cot_sem, out_sem,
    p_send, p_recv, a_send, a_recv, b_send, b_recv, y_send, y_recv, f_sem, x_send, x_recv, l_sem,
):
    arec, brec, yrec, frec = (arec0, arec1), (brec0, brec1), (yrec0, yrec1), (frec0, frec1)
    r = lax.axis_index("rep")
    f = lax.axis_index("fsdp")
    x, yl = r // 2, lax.rem(r, 2)
    yh, z, c = f // 16, lax.rem(f // 2, NZ), lax.rem(f, 2)

    def at(yh_, z_, c_):
        return (yh_ * NZ + z_) * 2 + c_

    pair = (r, at(yh, z, 1 - c))
    z_next = ((r, at(yh, lax.rem(z + 1, NZ), c)), (r, at(yh, lax.rem(z + NZ - 1, NZ), c)))
    y_peer = (r, at(1 - yh, z, c))
    x_next = ((lax.rem(x + 1, 4) * 2 + yl, f), (lax.rem(x + 3, 4) * 2 + yl, f))
    l_peer = (x * 2 + 1 - yl, f)

    def load_rows(src, dst, sem, k):
        for h in range(2):
            for jj in range(2):
                for yp in range(2):
                    zz = lax.rem(z + OFFSETS[2 * k + jj] + NZ, NZ)
                    cc = c if h else 1 - c
                    yy = yh if yp else 1 - yh
                    row = pl.multiple_of(at(yy, zz, cc) * 16, 16)
                    pltpu.make_async_copy(
                        src.at[pl.ds(row, 16), :],
                        dst.at[pl.ds(k * 128 + h * 64 + jj * 32 + yp * 16, 16), :],
                        sem.at[k],
                    ).start()

    def wait_rows(dst, sem, k):
        block = dst.at[pl.ds(k * 128, 128), :]
        pltpu.make_async_copy(block, block, sem.at[k]).wait()

    loads = [
        pltpu.make_async_copy(gain_hbm, gain, load_sem.at[0]),
        pltpu.make_async_copy(gate_hbm.at[0], wg, load_sem.at[1]),
        pltpu.make_async_copy(up_hbm.at[0], wu, load_sem.at[2]),
        pltpu.make_async_copy(down_hbm.at[0], wd, load_sem.at[3]),
        pltpu.make_async_copy(
            tokens.at[pl.ds(pl.multiple_of(f * 16, 16), 16), :], own_tok, load_sem.at[4]
        ),
        pltpu.make_async_copy(outer_hbm, outer, load_sem.at[5]),
        pltpu.make_async_copy(mom_hbm, mom, load_sem.at[6]),
    ]
    loads[0].start()
    load_rows(tokens, tok, tok_sem, 0)
    for i in (1, 2):
        loads[i].start()

    barrier = pltpu.get_barrier_semaphore()
    for other in (pair, *z_next, y_peer, *x_next, l_peer):
        pl.semaphore_signal(barrier, inc=1, device_id=other, device_id_type=MESH)

    loads[3].start()
    load_rows(tokens, tok, tok_sem, 1)
    load_rows(cot_hbm, cot, cot_sem, 0)
    for k in (2, 3):
        load_rows(tokens, tok, tok_sem, k)
    for k in (1, 2, 3):
        load_rows(cot_hbm, cot, cot_sem, k)
    for i in (4, 5, 6):
        loads[i].start()

    sends = []
    drained = [0]

    def remote(src, dst, ssem, rsem, to):
        copy = pltpu.make_async_remote_copy(
            src_ref=src, dst_ref=dst, send_sem=ssem, recv_sem=rsem, device_id=to, device_id_type=MESH
        )
        copy.start()
        sends.append(copy)
        return copy

    def drain(keep=16):
        until = max(drained[0], len(sends) - keep)
        for copy in sends[drained[0] : until]:
            copy.wait_send()
        drained[0] = until

    pairs, rings_a, rings_b, ys, finals, xs = {}, {}, {}, {}, {}, {}

    def pair_send(a, k, i):
        where = (a, pl.ds(k * 64, 64), pl.ds(*groups(a)[i]))
        pairs[a, k, i] = remote(
            peer.at[where], prec.at[where], p_send.at[a, k, i], p_recv.at[a, k, i], pair
        )

    def pair_add(a, k):
        for i in range(4):
            pairs[a, k, i].wait_recv()
            where = (a, pl.ds(k * 64, 64), pl.ds(*groups(a)[i]))
            own[where] += prec[where]

    def y_start(a, k):
        cols = pl.ds(2 * CA[a], 2 * CB[a])
        for j in (2 * k, 2 * k + 1):
            ys[a, j] = remote(
                own.at[a, pl.ds(j * 32, 16), cols], yrec[a].at[j],
                y_send.at[a, j], y_recv.at[a, j], y_peer,
            )

    def y_add(a, k):
        cols = pl.ds(2 * CA[a], 2 * CB[a])
        for j in (2 * k, 2 * k + 1):
            ys[a, j].wait_recv()
            own[a, pl.ds(j * 32 + 16, 16), cols] += yrec[a][j]

    def ring_a(a, step):
        for d in range(2):
            where = (a, pl.ds(slot_of(d, step) * 32, 32), pl.ds(*groups(a)[d]))
            if step:
                rings_a[a, d, step - 1].wait_recv()
                own[where] += arec[a][d, step - 1]
            if step < NZ - 1:
                rings_a[a, d, step] = remote(
                    own.at[where], arec[a].at[d, step], a_send.at[a, d, step], a_recv.at[a, d, step], z_next[d]
                )

    def ring_b(a, step):
        for d in range(2):
            where = (a, pl.ds(slot_of(d, step) * 32 + 16, 16), pl.ds(*groups(a)[2 + d]))
            if step:
                rings_b[a, d, step - 1].wait_recv()
                own[where] += brec[a][d, step - 1]
            if step < NZ - 1:
                rings_b[a, d, step] = remote(
                    own.at[where], brec[a].at[d, step], b_send.at[a, d, step], b_recv.at[a, d, step], z_next[d]
                )

    def final_start(a):
        ring_a(a, NZ - 1)
        finals[a] = remote(
            own.at[a, pl.ds(224, 16), pl.ds(0, 2 * CA[a])], frec[a], f_sem.at[0, a], f_sem.at[1, a], y_peer
        )

    def final_add(a):
        finals[a].wait_recv()
        own[a, pl.ds(240, 16), pl.ds(0, 2 * CA[a])] += frec[a][...]
        if a == 0:
            mixed_v[...] = (own[0, pl.ds(240, 16), :] * SCALE_OUT).astype(BF16)
            stores[0].start()

    def x_step(step):
        for d in range(2):
            if step:
                xs[d, step - 1].wait_recv()
                g[2 * step + d] += xrec[d, step - 1]
            if step < 3:
                xs[d, step] = remote(
                    g.at[2 * step + d], xrec.at[d, step], x_send.at[d, step], x_recv.at[d, step], x_next[d]
                )
        if step == 3:
            xs["l"] = remote(g.at[6], lrec, l_sem.at[0], l_sem.at[1], l_peer)

    def l_add():
        loads[5].wait()
        loads[6].wait()
        xs["l"].wait_recv()
        total = g[7] + lrec[...]
        held = outer[...]
        pseudo = held - total * (1.0 / N_REP)
        new_momentum = 0.9 * mom[...] + pseudo
        mom[...] = new_momentum
        outer[...] = held - 0.7 * (pseudo + 0.9 * new_momentum)
        stores[2].start()
        stores[3].start()

    stores = [
        pltpu.make_async_copy(mixed_v, mixed_out, out_sem.at[0]),
        pltpu.make_async_copy(grad_v, grad_out, out_sem.at[1]),
        pltpu.make_async_copy(outer, outer_out, out_sem.at[2]),
        pltpu.make_async_copy(mom, mom_out, out_sem.at[3]),
    ]

    def norm(k):
        wait_rows(tok, tok_sem, k)
        if k == 0:
            loads[0].wait()

        def some(i, carry):
            rows = pl.ds(pl.multiple_of(k * 128 + i * 16, 16), 16)
            part = tok[rows, :].astype(F32)
            inverse = lax.rsqrt(jnp.mean(part * part, axis=1, keepdims=True) + 1e-05)
            tok[rows, :] = (part * inverse * gain[...]).astype(BF16)
            return carry

        lax.fori_loop(0, 8, some, 0, unroll=2)

    def front(k):
        if k == 0:
            loads[1].wait()
            loads[2].wait()
        rows = pl.ds(k * 128, 128)
        normed = tok[rows, :]
        gate = lax.dot_general(normed, wg[...], NT, preferred_element_type=F32) * SCALE_IN
        up = lax.dot_general(normed, wu[...], NT, preferred_element_type=F32) * SCALE_IN
        gate_s[rows, :] = gate
        up_s[rows, :] = up
        sig = 1.0 / (1.0 + jnp.exp(-gate))
        hid[rows, :] = (gate * sig * up).astype(BF16)

    def put(a, k, value_of):
        for i, group in enumerate(groups(a)):
            for start, size in pieces(*group):
                cols = pl.ds(start, size)
                value = value_of(cols)
                peer[a, pl.ds(k * 64, 64), cols] = value[:64]
                own[a, pl.ds(k * 64, 64), cols] = value[64:]
            pair_send(a, k, i)

    def mix(k):
        if k == 0:
            loads[3].wait()
        hidden = hid[pl.ds(k * 128, 128), :]
        put(0, k, lambda cols: jnp.dot(hidden, wd[:, cols], preferred_element_type=F32))

    waited = set()

    def need_cot(k):
        if k not in waited:
            waited.add(k)
            wait_rows(cot, cot_sem, k)

    def back(k):
        need_cot(k)
        rows = pl.ds(k * 128, 128)
        d_hidden = lax.dot_general(cot[rows, :], wd[...], NT, preferred_element_type=F32) * SCALE_OUT
        gate = gate_s[rows, :]
        up = up_s[rows, :]
        sig = 1.0 / (1.0 + jnp.exp(-gate))
        d_gate = (d_hidden * up * sig * (1.0 + gate * (1.0 - sig))).astype(BF16)
        d_up = (d_hidden * (gate * sig)).astype(BF16)
        put(
            1, k,
            lambda cols: jnp.dot(d_gate, wg[:, cols], preferred_element_type=F32)
            + jnp.dot(d_up, wu[:, cols], preferred_element_type=F32),
        )

    def grad(q):
        if q == 0:
            hid_t[...] = hid[...].T
            for k in range(4):
                need_cot(k)
        step, side = q // 2, q % 2
        xx = lax.rem(x + 4 + (step + 1 if side else -(step + 1)), 4)
        col = pl.multiple_of((xx * 2 + (yl if side else 1 - yl)) * 512, 512)
        cols = pl.ds(col, 512)
        down_grad = jnp.dot(hid_t[...], cot[:, cols], preferred_element_type=F32)
        g[q] = wd[:, cols].astype(F32) - (0.5 * SCALE_OUT) * down_grad

    norm(0)
    front(0)
    pl.semaphore_wait(barrier, 7)
    mix(0)
    back(0)
    pair_add(0, 0)
    y_start(0, 0)
    ring_a(0, 0)
    norm(1)
    pair_add(1, 0)
    y_start(1, 0)
    ring_a(1, 0)
    front(1)
    mix(1)
    norm(2)
    norm(3)
    pair_add(0, 1)
    y_start(0, 1)
    ring_a(0, 1)
    y_add(0, 0)
    ring_b(0, 0)
    front(2)
    mix(2)
    front(3)
    pair_add(0, 2)
    ring_a(0, 2)
    y_start(0, 2)
    y_add(1, 0)
    ring_b(1, 0)
    mix(3)
    grad(0)
    grad(1)
    x_step(0)
    grad(2)
    grad(3)
    grad(4)
    grad(5)
    pair_add(0, 3)
    y_start(0, 3)
    ring_a(0, 3)
    y_add(0, 1)
    ring_b(0, 1)
    grad(6)
    grad(7)
    back(1)
    ring_a(0, 4)
    y_add(0, 2)
    pair_add(1, 1)
    y_start(1, 1)
    ring_b(0, 2)
    ring_a(1, 1)
    back(2)
    x_step(1)
    ring_a(0, 5)
    y_add(0, 3)
    ring_b(0, 3)
    pair_add(1, 2)
    y_start(1, 2)
    back(3)
    ring_a(1, 2)
    ring_a(0, 6)
    pair_add(1, 3)
    y_start(1, 3)
    ring_b(0, 4)
    y_add(1, 1)
    ring_b(1, 1)
    ring_a(1, 3)
    x_step(2)
    final_start(0)
    ring_b(0, 5)
    y_add(1, 2)
    ring_b(1, 2)
    drain()
    ring_a(1, 4)
    ring_b(0, 6)
    y_add(1, 3)
    ring_b(1, 3)
    drain()
    ring_a(1, 5)
    x_step(3)
    ring_b(0, 7)
    final_add(0)
    ring_b(1, 4)
    drain()
    ring_a(1, 6)
    ring_b(1, 5)
    drain()
    final_start(1)
    ring_b(1, 6)
    l_add()
    ring_b(1, 7)
    drain()
    final_add(1)

    loads[4].wait()
    part = own_tok[...].astype(F32)
    inverse = lax.rsqrt(jnp.mean(part * part, axis=1, keepdims=True) + 1e-05)
    plain = part * inverse
    scaled = own[1, pl.ds(240, 16), :] * SCALE_IN * gain[...]
    centre = jnp.mean(scaled * plain, axis=1, keepdims=True)
    grad_v[...] = (inverse * (scaled - plain * centre)).astype(BF16)
    stores[1].start()
    drain(0)
    for store in stores:
        store.wait()


def hand_on(*refs):
    held, sem = refs[8:12], refs[12]
    into = [pltpu.make_async_copy(refs[i], held[i], sem.at[0, i]) for i in range(4)]
    out = [pltpu.make_async_copy(held[i], refs[i + 4], sem.at[1, i]) for i in range(4)]
    for copy in into:
        copy.start()
    for i in range(4):
        into[i].wait()
        out[i].start()
    for copy in out:
        copy.wait()


def body(tokens, norm_gain, gate_weight, up_weight, down_weight, outer_block, momentum, cotangent):
    units = down_weight.shape[1]
    cols = outer_block.shape[1]
    hbm = pl.BlockSpec(memory_space=pl.ANY)
    dma = pltpu.SemaphoreType.DMA
    v = pltpu.VMEM
    results = (
        jax.ShapeDtypeStruct((16, D), BF16),
        jax.ShapeDtypeStruct((16, D), BF16),
        jax.ShapeDtypeStruct((units, cols), F32),
        jax.ShapeDtypeStruct((units, cols), F32),
    )
    made = pl.pallas_call(
        kernel,
        name="window",
        out_shape=results,
        in_specs=[hbm] * 8,
        out_specs=(hbm,) * 4,
        scratch_shapes=[
            v((512, D), BF16), v((512, D), BF16), v((units, D), BF16), v((units, D), BF16),
            v((units, D), BF16), v((1, D), F32), v((16, D), BF16), v((units, cols), F32), v((units, cols), F32),
            v((16, D), BF16), v((16, D), BF16),
            v((512, units), F32), v((512, units), F32), v((512, units), BF16), v((units, 512), BF16),
            v((2, 256, D), F32), v((2, 256, D), F32), v((2, 256, D), F32), v((8, units, cols), F32),
            v((2, 7, 32, CA[0]), F32), v((2, 7, 32, CA[1]), F32),
            v((2, 7, 16, CB[0]), F32), v((2, 7, 16, CB[1]), F32),
            v((8, 16, 2 * CB[0]), F32), v((8, 16, 2 * CB[1]), F32),
            v((16, 2 * CA[0]), F32), v((16, 2 * CA[1]), F32),
            v((2, 3, units, cols), F32), v((units, cols), F32),
            dma((7,)), dma((4,)), dma((4,)), dma((4,)),
            dma((2, 4, 4)), dma((2, 4, 4)), dma((2, 2, 7)), dma((2, 2, 7)), dma((2, 2, 7)), dma((2, 2, 7)),
            dma((2, 8)), dma((2, 8)), dma((2, 2)), dma((2, 3)), dma((2, 3)), dma((2,)),
        ],
        compiler_params=pltpu.CompilerParams(
            collective_id=0, has_side_effects=True, vmem_limit_bytes=63 * 2**20
        ),
    )(
        tokens, norm_gain.reshape(1, D), jnp.swapaxes(gate_weight, 1, 2), jnp.swapaxes(up_weight, 1, 2),
        down_weight, outer_block, momentum, cotangent,
    )
    return pl.pallas_call(
        hand_on,
        name="hand_on",
        out_shape=results,
        in_specs=[hbm] * 4,
        out_specs=(hbm,) * 4,
        scratch_shapes=[v(result.shape, result.dtype) for result in results] + [dma((2, 4))],
    )(*made)


def solution(mesh):
    placed = (
        P("rep", None),
        P(),
        P("rep", None, "fsdp"),
        P("rep", None, "fsdp"),
        P("rep", "fsdp", None),
        P("fsdp", "rep"),
        P("fsdp", "rep"),
        P("rep", None),
    )
    return jax.shard_map(
        body,
        mesh=mesh,
        in_specs=placed,
        out_specs=(
            P(("rep", "fsdp"), None),
            P(("rep", "fsdp"), None),
            P("fsdp", "rep"),
            P("fsdp", "rep"),
        ),
        check_vma=False,
    )
```

```python
import jax
import jax.numpy as jnp
from jax import lax
from jax.experimental import pallas as pl
from jax.experimental.pallas import tpu as pltpu
from jax.sharding import PartitionSpec as P

D = 4096
FFW = 7168
N_REP = 8
MESH = pl.DeviceIdType.MESH
F32 = jnp.float32
BF16 = jnp.bfloat16

NZ = 8
CA = (1024, 1024)
CB = (1024, 1024)
SCALE_IN = D ** (-0.5)
SCALE_OUT = FFW ** (-0.5)
NT = (((1,), (1,)), ((), ()))
OFFSETS = (-1, 1, -2, 2, -3, 3, 4, 0)


def groups(a):
    return ((0, CA[a]), (CA[a], CA[a]), (2 * CA[a], CB[a]), (2 * CA[a] + CB[a], CB[a]))


def pieces(start, size):
    return [(start + i, min(512, size - i)) for i in range(0, size, 512)]


def slot_of(direction, step):
    if step == NZ - 1:
        return 7
    if direction == 0:
        return 2 * step if step <= 3 else 13 - 2 * step
    return 2 * step + 1 if step <= 2 else 12 - 2 * step


def kernel(
    tokens, gain_hbm, gate_hbm, up_hbm, down_hbm, outer_hbm, mom_hbm, cot_hbm,
    mixed_out, grad_out, outer_out, mom_out,
    tok, cot, wg, wu, wd, gain, own_tok, outer, mom, mixed_v, grad_v,
    gate_s, up_s, hid, hid_t,
    own, peer, prec, g, arec0, arec1, brec0, brec1, yrec0, yrec1, frec0, frec1, xrec, lrec,
    load_sem, tok_sem, cot_sem, out_sem,
    p_send, p_recv, a_send, a_recv, b_send, b_recv, y_send, y_recv, f_sem, x_send, x_recv, l_sem,
):
    arec, brec, yrec, frec = (arec0, arec1), (brec0, brec1), (yrec0, yrec1), (frec0, frec1)
    r = lax.axis_index("rep")
    f = lax.axis_index("fsdp")
    x, yl = r // 2, lax.rem(r, 2)
    yh, z, c = f // 16, lax.rem(f // 2, NZ), lax.rem(f, 2)

    def at(yh_, z_, c_):
        return (yh_ * NZ + z_) * 2 + c_

    pair = (r, at(yh, z, 1 - c))
    z_next = ((r, at(yh, lax.rem(z + 1, NZ), c)), (r, at(yh, lax.rem(z + NZ - 1, NZ), c)))
    y_peer = (r, at(1 - yh, z, c))
    x_next = ((lax.rem(x + 1, 4) * 2 + yl, f), (lax.rem(x + 3, 4) * 2 + yl, f))
    l_peer = (x * 2 + 1 - yl, f)

    def load_rows(src, dst, sem, k):
        for h in range(2):
            for jj in range(2):
                for yp in range(2):
                    zz = lax.rem(z + OFFSETS[2 * k + jj] + NZ, NZ)
                    cc = c if h else 1 - c
                    yy = yh if yp else 1 - yh
                    row = pl.multiple_of(at(yy, zz, cc) * 16, 16)
                    pltpu.make_async_copy(
                        src.at[pl.ds(row, 16), :],
                        dst.at[pl.ds(k * 128 + h * 64 + jj * 32 + yp * 16, 16), :],
                        sem.at[k],
                    ).start()

    def wait_rows(dst, sem, k):
        block = dst.at[pl.ds(k * 128, 128), :]
        pltpu.make_async_copy(block, block, sem.at[k]).wait()

    loads = [
        pltpu.make_async_copy(gain_hbm, gain, load_sem.at[0]),
        pltpu.make_async_copy(gate_hbm.at[0], wg, load_sem.at[1]),
        pltpu.make_async_copy(up_hbm.at[0], wu, load_sem.at[2]),
        pltpu.make_async_copy(down_hbm.at[0], wd, load_sem.at[3]),
        pltpu.make_async_copy(
            tokens.at[pl.ds(pl.multiple_of(f * 16, 16), 16), :], own_tok, load_sem.at[4]
        ),
        pltpu.make_async_copy(outer_hbm, outer, load_sem.at[5]),
        pltpu.make_async_copy(mom_hbm, mom, load_sem.at[6]),
    ]
    loads[0].start()
    load_rows(tokens, tok, tok_sem, 0)
    for i in (1, 2):
        loads[i].start()

    barrier = pltpu.get_barrier_semaphore()
    for other in (pair, *z_next, y_peer, *x_next, l_peer):
        pl.semaphore_signal(barrier, inc=1, device_id=other, device_id_type=MESH)

    loads[3].start()
    load_rows(tokens, tok, tok_sem, 1)
    load_rows(cot_hbm, cot, cot_sem, 0)
    for k in (2, 3):
        load_rows(tokens, tok, tok_sem, k)
    for k in (1, 2, 3):
        load_rows(cot_hbm, cot, cot_sem, k)
    for i in (4, 5, 6):
        loads[i].start()

    sends = []
    drained = [0]

    def remote(src, dst, ssem, rsem, to):
        copy = pltpu.make_async_remote_copy(
            src_ref=src, dst_ref=dst, send_sem=ssem, recv_sem=rsem, device_id=to, device_id_type=MESH
        )
        copy.start()
        sends.append(copy)
        return copy

    def drain(keep=16):
        until = max(drained[0], len(sends) - keep)
        for copy in sends[drained[0] : until]:
            copy.wait_send()
        drained[0] = until

    pairs, rings_a, rings_b, ys, finals, xs = {}, {}, {}, {}, {}, {}

    def pair_send(a, k, i):
        where = (a, pl.ds(k * 64, 64), pl.ds(*groups(a)[i]))
        pairs[a, k, i] = remote(
            peer.at[where], prec.at[where], p_send.at[a, k, i], p_recv.at[a, k, i], pair
        )

    def pair_add(a, k):
        for i in range(4):
            pairs[a, k, i].wait_recv()
            where = (a, pl.ds(k * 64, 64), pl.ds(*groups(a)[i]))
            own[where] += prec[where]

    def y_start(a, step):
        for d in range(2):
            ys[a, d, step] = remote(
                own.at[a, pl.ds(slot_of(d, step) * 32, 16), pl.ds(*groups(a)[2 + d])], yrec[a].at[d, step],
                y_send.at[a, d, step], y_recv.at[a, d, step], y_peer,
            )

    def ring_a(a, step):
        for d in range(2):
            where = (a, pl.ds(slot_of(d, step) * 32, 32), pl.ds(*groups(a)[d]))
            if step:
                rings_a[a, d, step - 1].wait_recv()
                own[where] += arec[a][d, step - 1]
            if step < NZ - 1:
                rings_a[a, d, step] = remote(
                    own.at[where], arec[a].at[d, step], a_send.at[a, d, step], a_recv.at[a, d, step], z_next[d]
                )

    def ring_b(a, step):
        for d in range(2):
            where = (a, pl.ds(slot_of(d, step) * 32 + 16, 16), pl.ds(*groups(a)[2 + d]))
            ys[a, d, step].wait_recv()
            if step:
                rings_b[a, d, step - 1].wait_recv()
                own[where] += yrec[a][d, step] + brec[a][d, step - 1]
            else:
                own[where] += yrec[a][d, step]
            if step < NZ - 1:
                rings_b[a, d, step] = remote(
                    own.at[where], brec[a].at[d, step], b_send.at[a, d, step], b_recv.at[a, d, step], z_next[d]
                )

    def final_start(a):
        ring_a(a, NZ - 1)
        finals[a] = remote(
            own.at[a, pl.ds(224, 16), pl.ds(0, 2 * CA[a])], frec[a], f_sem.at[0, a], f_sem.at[1, a], y_peer
        )

    def final_add(a):
        finals[a].wait_recv()
        own[a, pl.ds(240, 16), pl.ds(0, 2 * CA[a])] += frec[a][...]
        if a == 0:
            mixed_v[...] = (own[0, pl.ds(240, 16), :] * SCALE_OUT).astype(BF16)
            stores[0].start()

    def x_step(step):
        for d in range(2):
            if step:
                xs[d, step - 1].wait_recv()
                g[2 * step + d] += xrec[d, step - 1]
            if step < 3:
                xs[d, step] = remote(
                    g.at[2 * step + d], xrec.at[d, step], x_send.at[d, step], x_recv.at[d, step], x_next[d]
                )
        if step == 3:
            xs["l"] = remote(g.at[6], lrec, l_sem.at[0], l_sem.at[1], l_peer)

    def l_add():
        loads[5].wait()
        loads[6].wait()
        xs["l"].wait_recv()
        total = g[7] + lrec[...]
        held = outer[...]
        pseudo = held - total * (1.0 / N_REP)
        new_momentum = 0.9 * mom[...] + pseudo
        mom[...] = new_momentum
        outer[...] = held - 0.7 * (pseudo + 0.9 * new_momentum)
        stores[2].start()
        stores[3].start()

    stores = [
        pltpu.make_async_copy(mixed_v, mixed_out, out_sem.at[0]),
        pltpu.make_async_copy(grad_v, grad_out, out_sem.at[1]),
        pltpu.make_async_copy(outer, outer_out, out_sem.at[2]),
        pltpu.make_async_copy(mom, mom_out, out_sem.at[3]),
    ]

    def norm(k):
        wait_rows(tok, tok_sem, k)
        if k == 0:
            loads[0].wait()

        def some(i, carry):
            rows = pl.ds(pl.multiple_of(k * 128 + i * 16, 16), 16)
            part = tok[rows, :].astype(F32)
            inverse = lax.rsqrt(jnp.mean(part * part, axis=1, keepdims=True) + 1e-05)
            tok[rows, :] = (part * inverse * gain[...]).astype(BF16)
            return carry

        lax.fori_loop(0, 8, some, 0, unroll=8)

    def front(k):
        if k == 0:
            loads[1].wait()
            loads[2].wait()
        rows = pl.ds(k * 128, 128)
        normed = tok[rows, :]
        gate = lax.dot_general(normed, wg[...], NT, preferred_element_type=F32) * SCALE_IN
        up = lax.dot_general(normed, wu[...], NT, preferred_element_type=F32) * SCALE_IN
        gate_s[rows, :] = gate
        up_s[rows, :] = up
        sig = 1.0 / (1.0 + jnp.exp(-gate))
        hid[rows, :] = (gate * sig * up).astype(BF16)

    def put(a, k, value_of):
        for i, group in enumerate(groups(a)):
            for start, size in pieces(*group):
                cols = pl.ds(start, size)
                value = value_of(cols)
                peer[a, pl.ds(k * 64, 64), cols] = value[:64]
                own[a, pl.ds(k * 64, 64), cols] = value[64:]
            pair_send(a, k, i)

    def mix(k):
        if k == 0:
            loads[3].wait()
        hidden = hid[pl.ds(k * 128, 128), :]
        put(0, k, lambda cols: jnp.dot(hidden, wd[:, cols], preferred_element_type=F32))

    waited = set()

    def need_cot(k):
        if k not in waited:
            waited.add(k)
            wait_rows(cot, cot_sem, k)

    def back(k):
        need_cot(k)
        rows = pl.ds(k * 128, 128)
        d_hidden = lax.dot_general(cot[rows, :], wd[...], NT, preferred_element_type=F32) * SCALE_OUT
        gate = gate_s[rows, :]
        up = up_s[rows, :]
        sig = 1.0 / (1.0 + jnp.exp(-gate))
        d_gate = (d_hidden * up * sig * (1.0 + gate * (1.0 - sig))).astype(BF16)
        d_up = (d_hidden * (gate * sig)).astype(BF16)
        put(
            1, k,
            lambda cols: jnp.dot(d_gate, wg[:, cols], preferred_element_type=F32)
            + jnp.dot(d_up, wu[:, cols], preferred_element_type=F32),
        )

    def grad(q):
        if q == 0:
            hid_t[...] = hid[...].T
            for k in range(4):
                need_cot(k)
        step, side = q // 2, q % 2
        xx = lax.rem(x + 4 + (step + 1 if side else -(step + 1)), 4)
        col = pl.multiple_of((xx * 2 + (yl if side else 1 - yl)) * 512, 512)
        cols = pl.ds(col, 512)
        down_grad = jnp.dot(hid_t[...], cot[:, cols], preferred_element_type=F32)
        g[q] = wd[:, cols].astype(F32) - (0.5 * SCALE_OUT) * down_grad

    norm(0)
    front(0)
    pl.semaphore_wait(barrier, 7)
    mix(0)
    back(0)
    norm(1)
    pair_add(0, 0)
    ring_a(0, 0)
    y_start(0, 0)
    front(1)
    pair_add(1, 0)
    ring_a(1, 0)
    y_start(1, 0)
    mix(1)
    norm(2)
    front(2)
    mix(2)
    pair_add(0, 1)
    ring_a(0, 1)
    y_start(0, 1)
    ring_b(0, 0)
    norm(3)
    front(3)
    pair_add(0, 2)
    y_start(0, 2)
    ring_b(1, 0)
    mix(3)
    ring_a(0, 2)
    grad(0)
    grad(1)
    x_step(0)
    grad(2)
    grad(3)
    grad(4)
    grad(5)
    grad(6)
    grad(7)
    ring_b(0, 1)
    pair_add(0, 3)
    y_start(0, 3)
    y_start(0, 4)
    y_start(0, 5)
    back(1)
    ring_a(0, 3)
    back(2)
    pair_add(1, 1)
    ring_a(1, 1)
    y_start(1, 1)
    ring_b(0, 2)
    y_start(0, 6)
    back(3)
    ring_a(0, 4)
    x_step(1)
    pair_add(1, 2)
    ring_a(1, 2)
    y_start(1, 2)
    pair_add(1, 3)
    y_start(1, 3)
    y_start(1, 4)
    ring_b(0, 3)
    y_start(0, 7)
    ring_b(1, 1)
    y_start(1, 5)
    ring_a(0, 5)
    ring_a(1, 3)
    ring_b(0, 4)
    ring_b(1, 2)
    y_start(1, 6)
    x_step(2)
    ring_a(0, 6)
    drain()
    ring_a(1, 4)
    ring_b(0, 5)
    ring_b(1, 3)
    y_start(1, 7)
    final_start(0)
    drain()
    ring_a(1, 5)
    x_step(3)
    ring_b(0, 6)
    ring_b(1, 4)
    drain()
    ring_a(1, 6)
    ring_b(0, 7)
    final_add(0)
    ring_b(1, 5)
    drain()
    final_start(1)
    ring_b(1, 6)
    l_add()
    ring_b(1, 7)
    drain()
    final_add(1)

    loads[4].wait()
    part = own_tok[...].astype(F32)
    inverse = lax.rsqrt(jnp.mean(part * part, axis=1, keepdims=True) + 1e-05)
    plain = part * inverse
    scaled = own[1, pl.ds(240, 16), :] * SCALE_IN * gain[...]
    centre = jnp.mean(scaled * plain, axis=1, keepdims=True)
    grad_v[...] = (inverse * (scaled - plain * centre)).astype(BF16)
    stores[1].start()
    drain(0)
    for store in stores:
        store.wait()


def hand_on(*refs):
    held, sem = refs[8:12], refs[12]
    into = [pltpu.make_async_copy(refs[i], held[i], sem.at[0, i]) for i in range(4)]
    out = [pltpu.make_async_copy(held[i], refs[i + 4], sem.at[1, i]) for i in range(4)]
    for copy in into:
        copy.start()
    for i in range(4):
        into[i].wait()
        out[i].start()
    for copy in out:
        copy.wait()


def body(tokens, norm_gain, gate_weight, up_weight, down_weight, outer_block, momentum, cotangent):
    units = down_weight.shape[1]
    cols = outer_block.shape[1]
    hbm = pl.BlockSpec(memory_space=pl.ANY)
    dma = pltpu.SemaphoreType.DMA
    v = pltpu.VMEM
    results = (
        jax.ShapeDtypeStruct((16, D), BF16),
        jax.ShapeDtypeStruct((16, D), BF16),
        jax.ShapeDtypeStruct((units, cols), F32),
        jax.ShapeDtypeStruct((units, cols), F32),
    )
    made = pl.pallas_call(
        kernel,
        name="window",
        out_shape=results,
        in_specs=[hbm] * 8,
        out_specs=(hbm,) * 4,
        scratch_shapes=[
            v((512, D), BF16), v((512, D), BF16), v((units, D), BF16), v((units, D), BF16),
            v((units, D), BF16), v((1, D), F32), v((16, D), BF16), v((units, cols), F32), v((units, cols), F32),
            v((16, D), BF16), v((16, D), BF16),
            v((512, units), F32), v((512, units), F32), v((512, units), BF16), v((units, 512), BF16),
            v((2, 256, D), F32), v((2, 256, D), F32), v((2, 256, D), F32), v((8, units, cols), F32),
            v((2, 7, 32, CA[0]), F32), v((2, 7, 32, CA[1]), F32),
            v((2, 7, 16, CB[0]), F32), v((2, 7, 16, CB[1]), F32),
            v((2, 8, 16, CB[0]), F32), v((2, 8, 16, CB[1]), F32),
            v((16, 2 * CA[0]), F32), v((16, 2 * CA[1]), F32),
            v((2, 3, units, cols), F32), v((units, cols), F32),
            dma((7,)), dma((4,)), dma((4,)), dma((4,)),
            dma((2, 4, 4)), dma((2, 4, 4)), dma((2, 2, 7)), dma((2, 2, 7)), dma((2, 2, 7)), dma((2, 2, 7)),
            dma((2, 2, 8)), dma((2, 2, 8)), dma((2, 2)), dma((2, 3)), dma((2, 3)), dma((2,)),
        ],
        compiler_params=pltpu.CompilerParams(
            collective_id=0, has_side_effects=True, vmem_limit_bytes=63 * 2**20
        ),
    )(
        tokens, norm_gain.reshape(1, D), jnp.swapaxes(gate_weight, 1, 2), jnp.swapaxes(up_weight, 1, 2),
        down_weight, outer_block, momentum, cotangent,
    )
    return pl.pallas_call(
        hand_on,
        name="hand_on",
        out_shape=results,
        in_specs=[hbm] * 4,
        out_specs=(hbm,) * 4,
        scratch_shapes=[v(result.shape, result.dtype) for result in results] + [dma((2, 4))],
    )(*made)


def solution(mesh):
    placed = (
        P("rep", None),
        P(),
        P("rep", None, "fsdp"),
        P("rep", None, "fsdp"),
        P("rep", "fsdp", None),
        P("fsdp", "rep"),
        P("fsdp", "rep"),
        P("rep", None),
    )
    return jax.shard_map(
        body,
        mesh=mesh,
        in_specs=placed,
        out_specs=(
            P(("rep", "fsdp"), None),
            P(("rep", "fsdp"), None),
            P("fsdp", "rep"),
            P("fsdp", "rep"),
        ),
        check_vma=False,
    )
```

```python
import jax
import jax.numpy as jnp
from jax import lax
from jax.experimental import pallas as pl
from jax.experimental.pallas import tpu as pltpu
from jax.sharding import PartitionSpec as P

D = 4096
FFW = 7168
N_REP = 8
MESH = pl.DeviceIdType.MESH
F32 = jnp.float32
BF16 = jnp.bfloat16

NZ = 8
CA = (1024, 1024)
CB = (1024, 1024)
SCALE_IN = D ** (-0.5)
SCALE_OUT = FFW ** (-0.5)
NT = (((1,), (1,)), ((), ()))
OFFSETS = (-1, 1, -2, 2, -3, 3, 4, 0)


def groups(a):
    return ((0, CA[a]), (CA[a], CA[a]), (2 * CA[a], CB[a]), (2 * CA[a] + CB[a], CB[a]))


def pieces(start, size):
    return [(start + i, min(512, size - i)) for i in range(0, size, 512)]


def slot_of(direction, step):
    if step == NZ - 1:
        return 7
    if direction == 0:
        return 2 * step if step <= 3 else 13 - 2 * step
    return 2 * step + 1 if step <= 2 else 12 - 2 * step


def kernel(
    tokens, gain_hbm, gate_hbm, up_hbm, down_hbm, outer_hbm, mom_hbm, cot_hbm,
    mixed_out, grad_out, outer_out, mom_out,
    tok, cot, wg, wu, wd, gain, own_tok, outer, mom, mixed_v, grad_v,
    gate_s, up_s, hid, hid_t,
    own, peer, prec, g, arec0, arec1, brec0, brec1, yrec0, yrec1, frec0, frec1, xrec, lrec,
    load_sem, tok_sem, cot_sem, out_sem,
    p_send, p_recv, a_send, a_recv, b_send, b_recv, y_send, y_recv, f_sem, x_send, x_recv, l_sem,
):
    arec, brec, yrec, frec = (arec0, arec1), (brec0, brec1), (yrec0, yrec1), (frec0, frec1)
    r = lax.axis_index("rep")
    f = lax.axis_index("fsdp")
    x, yl = r // 2, lax.rem(r, 2)
    yh, z, c = f // 16, lax.rem(f // 2, NZ), lax.rem(f, 2)

    def at(yh_, z_, c_):
        return (yh_ * NZ + z_) * 2 + c_

    pair = (r, at(yh, z, 1 - c))
    z_next = ((r, at(yh, lax.rem(z + 1, NZ), c)), (r, at(yh, lax.rem(z + NZ - 1, NZ), c)))
    y_peer = (r, at(1 - yh, z, c))
    x_next = ((lax.rem(x + 1, 4) * 2 + yl, f), (lax.rem(x + 3, 4) * 2 + yl, f))
    l_peer = (x * 2 + 1 - yl, f)

    def load_rows(src, dst, sem, k):
        for h in range(2):
            for jj in range(2):
                for yp in range(2):
                    zz = lax.rem(z + OFFSETS[2 * k + jj] + NZ, NZ)
                    cc = c if h else 1 - c
                    yy = yh if yp else 1 - yh
                    row = pl.multiple_of(at(yy, zz, cc) * 16, 16)
                    pltpu.make_async_copy(
                        src.at[pl.ds(row, 16), :],
                        dst.at[pl.ds(k * 128 + h * 64 + jj * 32 + yp * 16, 16), :],
                        sem.at[k],
                    ).start()

    def wait_rows(dst, sem, k):
        block = dst.at[pl.ds(k * 128, 128), :]
        pltpu.make_async_copy(block, block, sem.at[k]).wait()

    loads = [
        pltpu.make_async_copy(gain_hbm, gain, load_sem.at[0]),
        pltpu.make_async_copy(gate_hbm.at[0], wg, load_sem.at[1]),
        pltpu.make_async_copy(up_hbm.at[0], wu, load_sem.at[2]),
        pltpu.make_async_copy(down_hbm.at[0], wd, load_sem.at[3]),
        pltpu.make_async_copy(
            tokens.at[pl.ds(pl.multiple_of(f * 16, 16), 16), :], own_tok, load_sem.at[4]
        ),
        pltpu.make_async_copy(outer_hbm, outer, load_sem.at[5]),
        pltpu.make_async_copy(mom_hbm, mom, load_sem.at[6]),
    ]
    loads[0].start()
    load_rows(tokens, tok, tok_sem, 0)
    for i in (1, 2, 3):
        loads[i].start()
    load_rows(tokens, tok, tok_sem, 1)

    barrier = pltpu.get_barrier_semaphore()
    for other in (pair, *z_next, y_peer, *x_next, l_peer):
        pl.semaphore_signal(barrier, inc=1, device_id=other, device_id_type=MESH)

    load_rows(cot_hbm, cot, cot_sem, 0)
    for k in (2, 3):
        load_rows(tokens, tok, tok_sem, k)
    for k in (1, 2, 3):
        load_rows(cot_hbm, cot, cot_sem, k)
    for i in (4, 5, 6):
        loads[i].start()

    sends = []
    drained = [0]

    def remote(src, dst, ssem, rsem, to):
        copy = pltpu.make_async_remote_copy(
            src_ref=src, dst_ref=dst, send_sem=ssem, recv_sem=rsem, device_id=to, device_id_type=MESH
        )
        copy.start()
        sends.append(copy)
        return copy

    def drain(keep=16):
        until = max(drained[0], len(sends) - keep)
        for copy in sends[drained[0] : until]:
            copy.wait_send()
        drained[0] = until

    pairs, rings_a, rings_b, ys, finals, xs = {}, {}, {}, {}, {}, {}

    def pair_send(a, k, i):
        where = (a, pl.ds(k * 64, 64), pl.ds(*groups(a)[i]))
        pairs[a, k, i] = remote(
            peer.at[where], prec.at[where], p_send.at[a, k, i], p_recv.at[a, k, i], pair
        )

    def pair_add(a, k):
        for i in range(4):
            pairs[a, k, i].wait_recv()
            where = (a, pl.ds(k * 64, 64), pl.ds(*groups(a)[i]))
            own[where] += prec[where]

    def y_start(a, step):
        for d in range(2):
            ys[a, d, step] = remote(
                own.at[a, pl.ds(slot_of(d, step) * 32, 16), pl.ds(*groups(a)[2 + d])], yrec[a].at[d, step],
                y_send.at[a, d, step], y_recv.at[a, d, step], y_peer,
            )

    def ring_a(a, step):
        for d in range(2):
            where = (a, pl.ds(slot_of(d, step) * 32, 32), pl.ds(*groups(a)[d]))
            if step:
                rings_a[a, d, step - 1].wait_recv()
                own[where] += arec[a][d, step - 1]
            if step < NZ - 1:
                rings_a[a, d, step] = remote(
                    own.at[where], arec[a].at[d, step], a_send.at[a, d, step], a_recv.at[a, d, step], z_next[d]
                )

    def ring_b(a, step):
        for d in range(2):
            where = (a, pl.ds(slot_of(d, step) * 32 + 16, 16), pl.ds(*groups(a)[2 + d]))
            ys[a, d, step].wait_recv()
            if step:
                rings_b[a, d, step - 1].wait_recv()
                own[where] += yrec[a][d, step] + brec[a][d, step - 1]
            else:
                own[where] += yrec[a][d, step]
            if step < NZ - 1:
                rings_b[a, d, step] = remote(
                    own.at[where], brec[a].at[d, step], b_send.at[a, d, step], b_recv.at[a, d, step], z_next[d]
                )

    def final_start(a):
        ring_a(a, NZ - 1)
        finals[a] = remote(
            own.at[a, pl.ds(224, 16), pl.ds(0, 2 * CA[a])], frec[a], f_sem.at[0, a], f_sem.at[1, a], y_peer
        )

    def final_add(a):
        finals[a].wait_recv()
        own[a, pl.ds(240, 16), pl.ds(0, 2 * CA[a])] += frec[a][...]
        if a == 0:
            mixed_v[...] = (own[0, pl.ds(240, 16), :] * SCALE_OUT).astype(BF16)
            stores[0].start()

    def x_step(step):
        for d in range(2):
            if step:
                xs[d, step - 1].wait_recv()
                g[2 * step + d] += xrec[d, step - 1]
            if step < 3:
                xs[d, step] = remote(
                    g.at[2 * step + d], xrec.at[d, step], x_send.at[d, step], x_recv.at[d, step], x_next[d]
                )
        if step == 3:
            xs["l"] = remote(g.at[6], lrec, l_sem.at[0], l_sem.at[1], l_peer)

    def l_add():
        loads[5].wait()
        loads[6].wait()
        xs["l"].wait_recv()
        total = g[7] + lrec[...]
        held = outer[...]
        pseudo = held - total * (1.0 / N_REP)
        new_momentum = 0.9 * mom[...] + pseudo
        mom[...] = new_momentum
        outer[...] = held - 0.7 * (pseudo + 0.9 * new_momentum)
        stores[2].start()
        stores[3].start()

    stores = [
        pltpu.make_async_copy(mixed_v, mixed_out, out_sem.at[0]),
        pltpu.make_async_copy(grad_v, grad_out, out_sem.at[1]),
        pltpu.make_async_copy(outer, outer_out, out_sem.at[2]),
        pltpu.make_async_copy(mom, mom_out, out_sem.at[3]),
    ]

    def norm(k):
        wait_rows(tok, tok_sem, k)
        if k == 0:
            loads[0].wait()

        def some(i, carry):
            rows = pl.ds(pl.multiple_of(k * 128 + i * 16, 16), 16)
            part = tok[rows, :].astype(F32)
            inverse = lax.rsqrt(jnp.mean(part * part, axis=1, keepdims=True) + 1e-05)
            tok[rows, :] = (part * inverse * gain[...]).astype(BF16)
            return carry

        lax.fori_loop(0, 8, some, 0, unroll=8)

    def front(k):
        if k == 0:
            loads[1].wait()
            loads[2].wait()
        rows = pl.ds(k * 128, 128)
        normed = tok[rows, :]
        gate = lax.dot_general(normed, wg[...], NT, preferred_element_type=F32) * SCALE_IN
        up = lax.dot_general(normed, wu[...], NT, preferred_element_type=F32) * SCALE_IN
        gate_s[rows, :] = gate
        up_s[rows, :] = up
        sig = 1.0 / (1.0 + jnp.exp(-gate))
        hid[rows, :] = (gate * sig * up).astype(BF16)

    def put(a, k, value_of):
        for i, group in enumerate(groups(a)):
            for start, size in pieces(*group):
                cols = pl.ds(start, size)
                value = value_of(cols)
                peer[a, pl.ds(k * 64, 64), cols] = value[:64]
                own[a, pl.ds(k * 64, 64), cols] = value[64:]
            pair_send(a, k, i)

    def mix(k):
        if k == 0:
            loads[3].wait()
        hidden = hid[pl.ds(k * 128, 128), :]
        put(0, k, lambda cols: jnp.dot(hidden, wd[:, cols], preferred_element_type=F32))

    waited = set()

    def need_cot(k):
        if k not in waited:
            waited.add(k)
            wait_rows(cot, cot_sem, k)

    def back(k):
        need_cot(k)
        rows = pl.ds(k * 128, 128)
        d_hidden = lax.dot_general(cot[rows, :], wd[...], NT, preferred_element_type=F32) * SCALE_OUT
        gate = gate_s[rows, :]
        up = up_s[rows, :]
        sig = 1.0 / (1.0 + jnp.exp(-gate))
        d_gate = (d_hidden * up * sig * (1.0 + gate * (1.0 - sig))).astype(BF16)
        d_up = (d_hidden * (gate * sig)).astype(BF16)
        put(
            1, k,
            lambda cols: jnp.dot(d_gate, wg[:, cols], preferred_element_type=F32)
            + jnp.dot(d_up, wu[:, cols], preferred_element_type=F32),
        )

    def grad(q):
        if q == 0:
            hid_t[...] = hid[...].T
            for k in range(4):
                need_cot(k)
        step, side = q // 2, q % 2
        xx = lax.rem(x + 4 + (step + 1 if side else -(step + 1)), 4)
        col = pl.multiple_of((xx * 2 + (yl if side else 1 - yl)) * 512, 512)
        cols = pl.ds(col, 512)
        down_grad = jnp.dot(hid_t[...], cot[:, cols], preferred_element_type=F32)
        g[q] = wd[:, cols].astype(F32) - (0.5 * SCALE_OUT) * down_grad

    norm(0)
    front(0)
    pl.semaphore_wait(barrier, 7)
    mix(0)
    back(0)
    norm(1)
    pair_add(0, 0)
    ring_a(0, 0)
    y_start(0, 0)
    front(1)
    pair_add(1, 0)
    ring_a(1, 0)
    y_start(1, 0)
    mix(1)
    norm(2)
    front(2)
    mix(2)
    pair_add(0, 1)
    ring_a(0, 1)
    y_start(0, 1)
    ring_b(0, 0)
    norm(3)
    front(3)
    pair_add(0, 2)
    y_start(0, 2)
    ring_b(1, 0)
    mix(3)
    ring_a(0, 2)
    grad(0)
    grad(1)
    x_step(0)
    grad(2)
    grad(3)
    grad(4)
    grad(5)
    grad(6)
    grad(7)
    ring_b(0, 1)
    pair_add(0, 3)
    y_start(0, 3)
    y_start(0, 4)
    y_start(0, 5)
    back(1)
    ring_a(0, 3)
    back(2)
    pair_add(1, 1)
    ring_a(1, 1)
    y_start(1, 1)
    ring_b(0, 2)
    y_start(0, 6)
    back(3)
    ring_a(0, 4)
    x_step(1)
    pair_add(1, 2)
    ring_a(1, 2)
    y_start(1, 2)
    pair_add(1, 3)
    y_start(1, 3)
    y_start(1, 4)
    ring_b(0, 3)
    y_start(0, 7)
    ring_b(1, 1)
    y_start(1, 5)
    ring_a(0, 5)
    ring_a(1, 3)
    ring_b(0, 4)
    ring_b(1, 2)
    y_start(1, 6)
    x_step(2)
    ring_a(0, 6)
    drain()
    ring_a(1, 4)
    ring_b(0, 5)
    ring_b(1, 3)
    y_start(1, 7)
    final_start(0)
    drain()
    ring_a(1, 5)
    x_step(3)
    ring_b(0, 6)
    ring_b(1, 4)
    drain()
    ring_a(1, 6)
    ring_b(0, 7)
    final_add(0)
    ring_b(1, 5)
    drain()
    final_start(1)
    ring_b(1, 6)
    l_add()
    ring_b(1, 7)
    drain()
    final_add(1)

    loads[4].wait()
    part = own_tok[...].astype(F32)
    inverse = lax.rsqrt(jnp.mean(part * part, axis=1, keepdims=True) + 1e-05)
    plain = part * inverse
    scaled = own[1, pl.ds(240, 16), :] * SCALE_IN * gain[...]
    centre = jnp.mean(scaled * plain, axis=1, keepdims=True)
    grad_v[...] = (inverse * (scaled - plain * centre)).astype(BF16)
    stores[1].start()
    drain(0)
    for store in stores:
        store.wait()


def hand_on(*refs):
    held, sem = refs[8:12], refs[12]
    into = [pltpu.make_async_copy(refs[i], held[i], sem.at[0, i]) for i in range(4)]
    out = [pltpu.make_async_copy(held[i], refs[i + 4], sem.at[1, i]) for i in range(4)]
    for copy in into:
        copy.start()
    for i in range(4):
        into[i].wait()
        out[i].start()
    for copy in out:
        copy.wait()


def body(tokens, norm_gain, gate_weight, up_weight, down_weight, outer_block, momentum, cotangent):
    units = down_weight.shape[1]
    cols = outer_block.shape[1]
    hbm = pl.BlockSpec(memory_space=pl.ANY)
    dma = pltpu.SemaphoreType.DMA
    v = pltpu.VMEM
    results = (
        jax.ShapeDtypeStruct((16, D), BF16),
        jax.ShapeDtypeStruct((16, D), BF16),
        jax.ShapeDtypeStruct((units, cols), F32),
        jax.ShapeDtypeStruct((units, cols), F32),
    )
    made = pl.pallas_call(
        kernel,
        name="window",
        out_shape=results,
        in_specs=[hbm] * 8,
        out_specs=(hbm,) * 4,
        scratch_shapes=[
            v((512, D), BF16), v((512, D), BF16), v((units, D), BF16), v((units, D), BF16),
            v((units, D), BF16), v((1, D), F32), v((16, D), BF16), v((units, cols), F32), v((units, cols), F32),
            v((16, D), BF16), v((16, D), BF16),
            v((512, units), F32), v((512, units), F32), v((512, units), BF16), v((units, 512), BF16),
            v((2, 256, D), F32), v((2, 256, D), F32), v((2, 256, D), F32), v((8, units, cols), F32),
            v((2, 7, 32, CA[0]), F32), v((2, 7, 32, CA[1]), F32),
            v((2, 7, 16, CB[0]), F32), v((2, 7, 16, CB[1]), F32),
            v((2, 8, 16, CB[0]), F32), v((2, 8, 16, CB[1]), F32),
            v((16, 2 * CA[0]), F32), v((16, 2 * CA[1]), F32),
            v((2, 3, units, cols), F32), v((units, cols), F32),
            dma((7,)), dma((4,)), dma((4,)), dma((4,)),
            dma((2, 4, 4)), dma((2, 4, 4)), dma((2, 2, 7)), dma((2, 2, 7)), dma((2, 2, 7)), dma((2, 2, 7)),
            dma((2, 2, 8)), dma((2, 2, 8)), dma((2, 2)), dma((2, 3)), dma((2, 3)), dma((2,)),
        ],
        compiler_params=pltpu.CompilerParams(
            collective_id=0, has_side_effects=True, vmem_limit_bytes=63 * 2**20
        ),
    )(
        tokens, norm_gain.reshape(1, D), jnp.swapaxes(gate_weight, 1, 2), jnp.swapaxes(up_weight, 1, 2),
        down_weight, outer_block, momentum, cotangent,
    )
    return pl.pallas_call(
        hand_on,
        name="hand_on",
        out_shape=results,
        in_specs=[hbm] * 4,
        out_specs=(hbm,) * 4,
        scratch_shapes=[v(result.shape, result.dtype) for result in results] + [dma((2, 4))],
    )(*made)


def solution(mesh):
    placed = (
        P("rep", None),
        P(),
        P("rep", None, "fsdp"),
        P("rep", None, "fsdp"),
        P("rep", "fsdp", None),
        P("fsdp", "rep"),
        P("fsdp", "rep"),
        P("rep", None),
    )
    return jax.shard_map(
        body,
        mesh=mesh,
        in_specs=placed,
        out_specs=(
            P(("rep", "fsdp"), None),
            P(("rep", "fsdp"), None),
            P("fsdp", "rep"),
            P("fsdp", "rep"),
        ),
        check_vma=False,
    )
```
